256 devices in a mesh: order: 32 (over y_hi, z, core), member: 8 (over y_lo, x).
Axes of the slice: x: 4, y: 4 (y_hi: 2, y_lo: 2; y = y_hi * 2 + y_lo), z: 8, core: 2. Of those that a mesh axis runs over, the one named last changes fastest.
Arguments:
- members: bfloat16 [32, 384, 8, 2, 768], P('member', 'order'), may hold values from -5000 to 5000
- observed: bfloat16 [384, 8, 2, 768], P('order'), may hold values from -2000 to 2000
- pair_order: int32 [384], P('order'), may hold values from -1 to 360, as said below
- degree_weight: float32 [721], replicated, may hold values from 0.25 to 4
- cotangent: float32 [8], replicated, may hold values from 0.5 to 2
Outputs:
- member_grad: float32 [32, 384, 8, 2, 768], P('member', 'order')
The draws below stay inside these ranges and needn't reach their ends.
Inputs may be any that keep to these rules, and one draw needn't show every extreme that they name: `pair_order`: every shorter order 0 to 360 stands in exactly one row; the other 23 rows hold -1.
All inputs are finite; a program needn't handle non-finite values.
Results may differ from the reference program's by a relative error of at most 0.0012.
Values may be sent and summed in bfloat16 or wider, within the bound.
No kernel may reach another device: no remote copies, remote signals or barrier semaphores. Data moves between devices by JAX's collectives and lax.ppermute only.
A program may use at most 64 MiB of HBM per device.

```python
import math
import jax
import jax.numpy as jnp
from jax import lax

DEGREES = 721
CH = 8
MEM_DEV = 4
HALF = 361
PAIRS = 384
SLOTS = 768
MEMBERS = 32


def order_table(key):
    key = jax.random.fold_in(key, 11)
    row_index = jnp.arange(PAIRS, dtype=jnp.int32)
    values = jnp.where(row_index < HALF, row_index, -1).astype(jnp.int32)
    return jax.random.permutation(key, values).astype(jnp.int32)


def random_field(key, dims_shape):
    subkeys = jax.random.split(key, 1)
    gauss = jnp.clip(jax.random.normal(subkeys[0], dims_shape, jnp.float32), -5.0, 5.0)
    return gauss


def field_parts(key, spread):
    order_row = order_table(key)
    shorter = order_row[:, None]
    slot_index = lax.broadcasted_iota(jnp.int32, (PAIRS, SLOTS), 1)
    leading = slot_index < DEGREES - shorter
    degree = jnp.clip(jnp.where(leading, shorter + slot_index, slot_index - 1), 0, DEGREES - 1)
    degree_float = degree.astype(jnp.float32)
    falloff = 1.0 / (1.0 + degree_float / (DEGREES // 8))
    ramp = (degree_float / (DEGREES - 1)) ** 2
    key = jax.random.fold_in(key, 5)
    subkeys = jax.random.split(key, 3)
    row_factor = jnp.exp(spread * jax.random.uniform(subkeys[0], (PAIRS, CH, 1, 1), jnp.float32))
    slot_factor = jnp.exp(spread * jax.random.uniform(subkeys[1], (1, 1, 1, SLOTS), jnp.float32))
    base = row_factor * slot_factor
    amplitude = base * falloff[:, None, None, :]
    common = random_field(subkeys[2], (PAIRS, CH, 2, SLOTS))
    return (amplitude, common, base, ramp)


def draw_members(key, part):
    spread = math.log(10.0)
    amplitude, common, base, ramp = field_parts(key, spread)
    key = jax.random.fold_in(key, 7)
    subkeys = jax.random.split(key, 4)
    cluster_slot = jnp.exp(jax.random.uniform(subkeys[0], (PAIRS, 1, 1, SLOTS), jnp.float32, math.log(0.5), math.log(2.0)))
    cluster_profile = base * ramp[:, None, None, :] * cluster_slot
    member_scale = jnp.exp(jax.random.uniform(subkeys[2], (MEMBERS, 1, CH, 1, 1), jnp.float32, math.log(0.5), math.log(2.0)))

    def one_member(index):
        group = index // MEM_DEV
        group_keys = jax.random.split(jax.random.fold_in(subkeys[1], group), 2)
        cluster_gain = jnp.exp(jax.random.uniform(group_keys[0], (1, CH, 1, 1), jnp.float32, math.log(0.5), math.log(2.0)))
        offset = cluster_gain * cluster_profile * random_field(group_keys[1], (PAIRS, CH, 2, SLOTS))
        spread_part = random_field(jax.random.fold_in(subkeys[3], index), (PAIRS, CH, 2, SLOTS))
        scaling = lax.dynamic_index_in_dim(member_scale, index, 0, keepdims=False)
        return (amplitude * (common + scaling * spread_part) + offset).astype(jnp.bfloat16)
    return lax.map(one_member, jnp.arange(MEMBERS, dtype=jnp.int32))


def draw_observed(key, part):
    spread = math.log(10.0)
    amplitude, common, base, ramp = field_parts(key, spread)
    key = jax.random.fold_in(key, 9)
    own_part = random_field(key, (PAIRS, CH, 2, SLOTS))
    return (amplitude * (common + own_part)).astype(jnp.bfloat16)


def draw_pair_order(key, part):
    return order_table(key)


def setup_inputs(seed: int = 0) -> dict:
    streams_of = jax.random.split(jax.random.key(seed), 6)
    return {
        "members": draw_members(jax.random.fold_in(streams_of[5], 71), 0),
        "observed": draw_observed(jax.random.fold_in(streams_of[5], 71), 0),
        "pair_order": draw_pair_order(jax.random.fold_in(streams_of[5], 71), 0),
        "degree_weight": jnp.clip(jnp.exp(jax.random.uniform(streams_of[3], (DEGREES,), jnp.float32, math.log(0.25), math.log(4.0))), 0.25, 4.0),
        "cotangent": jnp.clip(jax.random.uniform(streams_of[4], (CH,), jnp.float32, 0.5, 2.0), 0.5, 2.0),
    }


epsilon = 1e-06

def slot_weights(pair_order, degree_weight, slot_count):
    degrees = degree_weight.shape[0]
    slot_index = lax.broadcasted_iota(jnp.int32, (pair_order.shape[0], slot_count), 1)
    shorter = pair_order[:, None]
    leading = slot_index < degrees - shorter
    padded = jnp.concatenate([degree_weight, jnp.zeros((slot_count,), jnp.float32)])
    starts = jnp.maximum(pair_order, 0).astype(jnp.int32)
    head_part = jax.vmap(lambda start: lax.dynamic_slice_in_dim(padded, start, slot_count))(starts)
    tail_part = jnp.concatenate([jnp.zeros((1,), jnp.float32), degree_weight, jnp.zeros((slot_count - degrees - 1,), jnp.float32)])[None, :]
    usable = (shorter >= 0) & (leading | (slot_index <= degrees) & (2 * shorter < degrees - 1))
    multiplicity = jnp.where(leading & (shorter == 0), 1.0, 2.0)
    return jnp.where(usable, jnp.where(leading, head_part, tail_part) * multiplicity, 0.0)

def reference(members, observed, pair_order, degree_weight, cotangent):
    weights = slot_weights(pair_order, degree_weight, members.shape[-1])[:, None, None, :]
    target = observed.astype(jnp.float32)
    total_members = members.shape[0]

    def weighted_square(leading, partner):
        difference = leading - partner
        return lax.optimization_barrier(jnp.sum(weights * difference * difference, axis=(0, 2, 3)))
    target_sq = lax.map(lambda member: weighted_square(member.astype(jnp.float32), target), members)

    def pair_row(member):
        leading = member.astype(jnp.float32)
        return lax.map(lambda partner: weighted_square(leading, partner.astype(jnp.float32)), members)
    pair_sq = lax.map(pair_row, members)
    target_dist = jnp.sqrt(target_sq + epsilon)
    keep_mask = 1.0 - jnp.eye(total_members, dtype=jnp.float32)[:, :, None]
    factor = keep_mask / jnp.sqrt(pair_sq + epsilon) / (total_members - 1)
    degrees = degree_weight.shape[0]

    def gradient_row(member_index):
        leading = members[member_index].astype(jnp.float32)

        def accumulate(pulled, partner_index):
            difference = leading - members[partner_index].astype(jnp.float32)
            return (pulled + factor[member_index, partner_index][None, :, None, None] * difference, None)
        pulled, _ = lax.scan(accumulate, jnp.zeros_like(leading), jnp.arange(total_members, dtype=jnp.int32))
        toward = (leading - target) / target_dist[member_index][None, :, None, None]
        return degrees * cotangent[None, :, None, None] * weights * (toward - pulled)
    return lax.map(gradient_row, jnp.arange(total_members, dtype=jnp.int32))
```

```python
import functools

import jax
import jax.numpy as jnp
from jax import lax
from jax.experimental import pallas as pl
from jax.experimental.pallas import tpu as pltpu
from jax.sharding import PartitionSpec as P

epsilon = 1e-06
LANES = 128
GROUP = 4
BATCH = 32


def pair_table(count):
    groups = [list(range(g, g + GROUP)) for g in range(0, count, GROUP)]
    cross = [(a, b) for a in range(len(groups)) for b in range(a + 1, len(groups))]
    batches = []
    for at in range(0, len(cross), 2):
        batches.append([(m, n) for a, b in cross[at : at + 2] for m in groups[a] for n in groups[b]])
    for at in range(0, len(groups), 2):
        inner = [(m, n) for g in groups[at : at + 2] for i, m in enumerate(g) for n in g[i + 1 :]]
        batches.append(inner + [(m, count) for g in groups[at : at + 2] for m in g])
    place, start, starts = {}, 0, []
    for batch in batches:
        starts.append(start)
        for index, pair in enumerate(batch):
            place[pair] = start + index
        start += -(-len(batch) // 8) * 8
    return batches, starts, place, -(-start // LANES) * LANES


def fold_rows(blocks):
    row = lax.broadcasted_iota(jnp.int32, (8, LANES), 0)
    for half in (4, 2, 1):
        low = (row & half) == 0
        count = len(blocks) // 2
        merged = []
        for i in range(count):
            a, b = blocks[i], blocks[i + count]
            kept = jnp.where(low, a, b)
            moved = jnp.where(low, b, a)
            merged.append(kept + (pltpu.roll(moved, half, 0) if half == 4 else swap(moved, half, low)))
        blocks = merged
    return blocks[0]


def swap(block, half, low):
    return jnp.where(low, pltpu.roll(block, 8 - half, 0), pltpu.roll(block, half, 0))


def weights_kernel(degrees, order_ref, table_ref, out_ref):
    slots = table_ref.shape[1]
    parts = slots // LANES
    table = table_ref[...]
    slot = lax.broadcasted_iota(jnp.int32, table.shape, 1)
    tail = pltpu.roll(table, 1, 1)
    for row in range(order_ref.shape[0]):
        order = order_ref[row]
        head = pltpu.roll(table, lax.rem(slots - jnp.maximum(order, 0), slots), 1)
        leading = slot < degrees - order
        second = (slot <= degrees) & (2 * order < degrees - 1)
        usable = (order >= 0) & (leading | second)
        times = jnp.where(leading & (order == 0), 1.0, 2.0)
        line = jnp.where(usable, jnp.where(leading, head, tail) * times, 0.0)
        for part in range(parts):
            at = (row * parts + part) * 2
            out_ref[at : at + 2, :] = line[0:2, part * LANES : (part + 1) * LANES]


def distance_kernel(batches, starts, count, x_ref, y_ref, w_ref, out_ref, scaled_ref, sums_ref):
    rows = w_ref.shape[0]

    def scale(i, carry):
        at = pl.ds(pl.multiple_of(i * 16, 16), 16)
        root = jnp.sqrt(w_ref[at, :])
        for m in range(count):
            scaled_ref[m, at, :] = x_ref[m, at, :].astype(jnp.float32) * root
        scaled_ref[count, at, :] = y_ref[at, :].astype(jnp.float32) * root
        return carry

    lax.fori_loop(0, rows // 16, scale, 0)
    sums_ref[...] = jnp.zeros_like(sums_ref)
    for batch, start in zip(batches, starts):
        used = sorted({m for pair in batch for m in pair})

        def add(i, sums, batch=batch, used=used):
            at = pl.ds(pl.multiple_of(i * 8, 8), 8)
            held = {m: scaled_ref[m, at, :] for m in used}
            out = []
            for (m, n), total in zip(batch, sums):
                difference = held[m] - held[n]
                out.append(total + difference * difference)
            return tuple(out)

        zero = jnp.zeros((8, LANES), jnp.float32)
        sums = list(lax.fori_loop(0, rows // 8, add, (zero,) * len(batch)))
        sums += [zero] * (-len(sums) % 8)
        for at in range(0, len(sums), 8):
            sums_ref[start + at : start + at + 8, :] = fold_rows(sums[at : at + 8])
    out_ref[...] = jnp.zeros_like(out_ref)
    for block in range(sums_ref.shape[0] // LANES):
        square = sums_ref[block * LANES : (block + 1) * LANES, :].T
        out_ref[block : block + 1, :] = jnp.sum(square, axis=0, keepdims=True)


def gradient_kernel(place, count, got_ref, x_ref, y_ref, w_ref, c_ref, out_ref, table_ref, wide_ref, pull_ref):
    rows = w_ref.shape[0]
    squares = jnp.sum(got_ref[...], axis=0)
    inverse = lax.rsqrt(squares + epsilon)
    columns = inverse.T
    for block in range(table_ref.shape[0] // LANES):
        column = jnp.broadcast_to(columns[:, block : block + 1], (LANES, LANES))
        table_ref[block * LANES : (block + 1) * LANES, :] = column

    def entry(m, n):
        at = place[(min(m, n), max(m, n))]
        return jnp.broadcast_to(table_ref[at : at + 1, :], (16, LANES))

    def slab(i, carry):
        at = pl.ds(pl.multiple_of(i * 16, 16), 16)
        for m in range(count):
            wide_ref[m] = x_ref[m, at, :].astype(jnp.float32)
        target = y_ref[at, :].astype(jnp.float32)
        weight = w_ref[at, :] * c_ref[0]
        share = 1.0 / (count - 1)
        for first in range(0, count, GROUP):
            own = list(range(first, first + GROUP))
            held = [wide_ref[m] for m in own]
            if first == 0:
                pulls = [jnp.zeros((16, LANES), jnp.float32) for _ in own]
            else:
                pulls = [pull_ref[m] for m in own]
            for i_m in range(GROUP):
                for i_n in range(i_m + 1, GROUP):
                    term = entry(own[i_m], own[i_n]) * (held[i_m] - held[i_n])
                    pulls[i_m] += term
                    pulls[i_n] -= term
            for second in range(first + GROUP, count, GROUP):
                for n in range(second, second + GROUP):
                    partner = wide_ref[n]
                    back = jnp.zeros((16, LANES), jnp.float32) if first == 0 else pull_ref[n]
                    for i_m in range(GROUP):
                        term = entry(own[i_m], n) * (held[i_m] - partner)
                        pulls[i_m] += term
                        back -= term
                    pull_ref[n] = back
            for i_m in range(GROUP):
                toward = (held[i_m] - target) * entry(own[i_m], count)
                out_ref[own[i_m], at, :] = (weight * (toward - pulls[i_m] * share)).astype(out_ref.dtype)
        return carry

    lax.fori_loop(0, rows // 16, slab, 0)


def on_device(members, observed, pair_order, degree_weight, cotangent):
    groups = lax.axis_size("member")
    spread = lax.axis_size("order")
    local, lines, channels, parts, slots = members.shape
    count = local * groups
    tiles = slots // LANES
    rows = lines * parts * tiles
    degrees = degree_weight.shape[0]
    batches, starts, place, entries = pair_table(count)
    vmem = pltpu.CompilerParams(vmem_limit_bytes=48 << 20)

    table = jnp.broadcast_to(jnp.pad(degree_weight, (0, slots - degrees))[None], (8, slots))
    weights = pl.pallas_call(
        functools.partial(weights_kernel, degrees),
        out_shape=jax.ShapeDtypeStruct((rows, LANES), jnp.float32),
        in_specs=[pl.BlockSpec(memory_space=pltpu.SMEM), pl.BlockSpec(memory_space=pltpu.VMEM)],
        compiler_params=vmem,
        name="slot_weights",
    )(pair_order, table)

    channel = lax.axis_index("member")
    held = lax.all_to_all(members.transpose(2, 0, 1, 3, 4), "member", 0, 0, tiled=True)
    held = held.reshape(count, lines, parts, tiles, LANES).transpose(0, 1, 3, 2, 4).reshape(count, rows, LANES)
    target = lax.dynamic_index_in_dim(observed, channel, 1, keepdims=False)
    target = target.reshape(lines, parts, tiles, LANES).transpose(0, 2, 1, 3).reshape(rows, LANES)

    blocks = entries // LANES
    sums = pl.pallas_call(
        functools.partial(distance_kernel, batches, starts, count),
        out_shape=jax.ShapeDtypeStruct((8, LANES), jnp.float32),
        scratch_shapes=[
            pltpu.VMEM((count + 1, rows, LANES), jnp.float32),
            pltpu.VMEM((entries, LANES), jnp.float32),
        ],
        compiler_params=vmem,
        name="distances",
    )(held, target, weights)
    got = lax.all_to_all(jnp.broadcast_to(sums[None], (spread, 8, LANES)), "order", 0, 0, tiled=True)

    factor = lax.dynamic_slice_in_dim(cotangent, channel, 1) * degrees
    whole = pl.BlockSpec(memory_space=pltpu.VMEM)
    gradient = pl.pallas_call(
        functools.partial(gradient_kernel, place, count),
        out_shape=jax.ShapeDtypeStruct((count, rows, LANES), jnp.float32),
        in_specs=[whole, whole, whole, whole, pl.BlockSpec(memory_space=pltpu.SMEM)],
        scratch_shapes=[
            pltpu.VMEM((blocks * LANES, LANES), jnp.float32),
            pltpu.VMEM((count, 16, LANES), jnp.float32),
            pltpu.VMEM((count, 16, LANES), jnp.float32),
        ],
        compiler_params=vmem,
        name="gradients",
    )(got, held, target, weights, factor)

    back = gradient.reshape(groups, local, lines, tiles, parts, LANES).transpose(0, 1, 2, 4, 3, 5)
    back = lax.all_to_all(back.reshape(groups, local, lines, parts, slots), "member", 0, 0, tiled=True)
    return back.transpose(1, 2, 0, 3, 4)


def solution(mesh):
    placed = (
        P("member", "order", None, None, None),
        P("order", None, None, None),
        P("order"),
        P(),
        P(),
    )
    return jax.shard_map(
        on_device,
        mesh=mesh,
        in_specs=placed,
        out_specs=P("member", "order", None, None, None),
        check_vma=False,
    )
```

```python
import functools

import jax
import jax.numpy as jnp
from jax import lax
from jax.experimental import pallas as pl
from jax.experimental.layout import Layout, with_layout_constraint
from jax.experimental.pallas import tpu as pltpu
from jax.sharding import PartitionSpec as P

epsilon = 1e-06
LANES = 128
GROUP = 4
BATCH = 32
POWER = 13.0


def pair_table(stages, local, count):
    members_of = [list(range(g * local, (g + 1) * local)) for g in range(count // local)]
    plans, place, start = [], {}, 0
    for stage in stages:
        cross = [(a, b) for b in stage for a in range(b)]
        lists = [
            [(m, n) for a, b in cross[at : at + 2] for m in members_of[a] for n in members_of[b]]
            for at in range(0, len(cross), 2)
        ]
        for at in range(0, len(stage), 2):
            own = [members_of[g] for g in stage[at : at + 2]]
            inner = [(m, n) for g in own for i, m in enumerate(g) for n in g[i + 1 :]]
            lists.append(inner + [(m, count) for g in own for m in g])
        if len(lists) > 1 and len(lists[-1]) + len(lists[-2]) <= BATCH:
            lists[-2:] = [lists[-2] + lists[-1]]
        plan, first = [], start
        for batch in lists:
            plan.append((batch, start - first))
            for index, pair in enumerate(batch):
                place[pair] = start + index
            start += -(-len(batch) // 8) * 8
        start = -(-start // LANES) * LANES
        plans.append((plan, (start - first) // LANES))
    return plans, place, start


def fold_rows(blocks):
    row = lax.broadcasted_iota(jnp.int32, (8, LANES), 0)
    for half in (4, 2, 1):
        low = (row & half) == 0
        count = len(blocks) // 2
        merged = []
        for i in range(count):
            a, b = blocks[i], blocks[i + count]
            kept = jnp.where(low, a, b)
            moved = jnp.where(low, b, a)
            merged.append(kept + (pltpu.roll(moved, half, 0) if half == 4 else swap(moved, half, low)))
        blocks = merged
    return blocks[0]


def swap(block, half, low):
    return jnp.where(low, pltpu.roll(block, 8 - half, 0), pltpu.roll(block, half, 0))


def prepare_kernel(degrees, shifts, x_ref, y_ref, order_from, table_from, c_from, *refs):
    *out_refs, target_ref, weight_ref, drawn_ref, near_ref, order_ref, table_ref, c_ref, in_sems, out_sems, sems = refs
    local = near_ref.shape[0]
    me = lax.axis_index("member")
    into = [pltpu.make_async_copy(x_ref.at[m], near_ref.at[m], in_sems.at[m]) for m in range(local)]
    small = [
        pltpu.make_async_copy(order_from, order_ref, sems.at[0]),
        pltpu.make_async_copy(table_from, table_ref, sems.at[1]),
        pltpu.make_async_copy(c_from, c_ref, sems.at[2]),
        pltpu.make_async_copy(y_ref.at[:, me], target_ref, sems.at[3]),
    ]
    for copy in into + small:
        copy.start()
    out = []
    for m in range(local):
        into[m].wait()
        for step, shift in enumerate(shifts):
            channel = jnp.bitwise_xor(me, shift)
            copy = pltpu.make_async_copy(near_ref.at[m, :, channel], out_refs[step].at[m], out_sems.at[m, step])
            copy.start()
            out.append(copy)
    for copy in small:
        copy.wait()

    parts = target_ref.shape[-1] // LANES
    slots = parts * LANES
    line = table_ref[...].reshape(1, degrees)
    line = jnp.concatenate([line, jnp.zeros((1, slots - degrees), jnp.float32)], axis=1)
    table = jnp.broadcast_to(line, (8, slots))
    slot = lax.broadcasted_iota(jnp.int32, table.shape, 1)
    tail = pltpu.roll(table, 1, 1)
    half = 0.5 * c_ref[me]
    for row in range(order_ref.shape[0]):
        order = order_ref[row]
        head = pltpu.roll(table, lax.rem(slots - jnp.maximum(order, 0), slots), 1)
        leading = slot < degrees - order
        second = (slot <= degrees) & (2 * order < degrees - 1)
        usable = (order >= 0) & (leading | second)
        times = jnp.where(leading & (order == 0), 1.0, 2.0)
        line = jnp.where(usable, jnp.where(leading, head, tail) * times, 0.0)
        for part in range(parts):
            at = (row * parts + part) * 2
            piece = line[0:2, part * LANES : (part + 1) * LANES]
            weight_ref[at : at + 2, :] = piece
            drawn_ref[at : at + 2, :] = piece * half
    for copy in out:
        copy.wait()


def distance_kernel(plan, blocks, fresh, earlier, with_target, last, *refs):
    refs = list(refs)
    old_refs = [refs.pop(0) for _ in range(blocks)]
    new_refs = [refs.pop(0) for _ in range(fresh)]
    y_ref, w_ref = refs.pop(0), refs.pop(0)
    before = [refs.pop(0) for _ in range(earlier)]
    line_ref = refs.pop(0)
    scaled_refs = [refs.pop(0) for _ in range(fresh)]
    target_ref = refs.pop(0) if with_target else y_ref
    sums_ref = refs.pop(0)
    rows = w_ref.shape[0]
    local = new_refs[0].shape[0]

    def scale(i, carry):
        at = pl.ds(pl.multiple_of(i * 16, 16), 16)
        root = jnp.sqrt(w_ref[at, :])
        for x_ref, scaled_ref in zip(new_refs, scaled_refs):
            for m in range(local):
                scaled_ref[m, at, :] = x_ref[m, at, :].astype(jnp.float32) * root
        if with_target:
            target_ref[at, :] = y_ref[at, :].astype(jnp.float32) * root
        return carry

    lax.fori_loop(0, rows // 16, scale, 0)
    every = old_refs + scaled_refs

    def piece(m, at):
        if m // local < blocks + fresh:
            return every[m // local][m % local, at : at + 8, :]
        return target_ref[at : at + 8, :]

    zero = jnp.zeros((8, LANES), jnp.float32)
    sums_ref[...] = jnp.zeros_like(sums_ref)
    for batch, start in plan:
        used = sorted({m for pair in batch for m in pair})
        sums = [zero] * len(batch)
        for at in range(0, rows, 8):
            held = {m: piece(m, at) for m in used}
            for index, (m, n) in enumerate(batch):
                difference = held[m] - held[n]
                sums[index] = sums[index] + difference * difference
        sums += [zero] * (-len(sums) % 8)
        for at in range(0, len(sums), 8):
            sums_ref[start + at : start + at + 8, :] = fold_rows(sums[at : at + 8])
    to = 0
    if last:
        line_ref[...] = jnp.zeros_like(line_ref)
        for ref in before:
            line_ref[to : to + ref.shape[0], :] = ref[...]
            to += ref.shape[0]
    for block in range(sums_ref.shape[0] // LANES):
        square = sums_ref[block * LANES : (block + 1) * LANES, :].T
        line_ref[to + block : to + block + 1, :] = jnp.sum(square, axis=0, keepdims=True)


def gradient_kernel(place, count, shifts, got_ref, *refs):
    *x_refs, y_ref, w_ref, out_ref, table_ref, wide_ref, pull_ref = refs
    rows = w_ref.shape[0]
    groups = out_ref.shape[0]
    local = count // groups
    slot = [jnp.bitwise_xor(lax.axis_index("member"), shift) for shift in shifts]
    squares = jnp.sum(got_ref[...], axis=0)
    inverse = lax.rsqrt(squares + epsilon)
    largest = jnp.max(squares * inverse * inverse, axis=(0, 1), keepdims=True)
    power = POWER + jnp.floor(jnp.clip(-0.5 * jnp.log2(jnp.maximum(largest, 1e-30)), 0.0, 50.0))
    scale = jnp.broadcast_to(jnp.exp2(power), (16, LANES))
    for group in range(out_ref.shape[0]):
        out_ref[group, local * rows :, :] = jnp.broadcast_to(power, (16, LANES))
    columns = inverse.T
    for block in range(table_ref.shape[0] // LANES):
        column = jnp.broadcast_to(columns[:, block : block + 1], (LANES, LANES))
        table_ref[block * LANES : (block + 1) * LANES, :] = column

    def entry(m, n):
        at = place[(min(m, n), max(m, n))]
        return jnp.broadcast_to(table_ref[at : at + 1, :], (16, LANES))

    def slab(i, carry):
        at = pl.ds(pl.multiple_of(i * 16, 16), 16)
        for m in range(count):
            wide_ref[m] = x_refs[m // local][m % local, at, :].astype(jnp.float32)
        target = y_ref[at, :].astype(jnp.float32)
        weight = w_ref[at, :] * scale
        share = 1.0 / (count - 1)
        for first in range(0, count, GROUP):
            own = list(range(first, first + GROUP))
            held = [wide_ref[m] for m in own]
            if first == 0:
                pulls = [jnp.zeros((16, LANES), jnp.float32) for _ in own]
            else:
                pulls = [pull_ref[m] for m in own]
            for i_m in range(GROUP):
                for i_n in range(i_m + 1, GROUP):
                    term = entry(own[i_m], own[i_n]) * (held[i_m] - held[i_n])
                    pulls[i_m] += term
                    pulls[i_n] -= term
            for second in range(first + GROUP, count, GROUP):
                for n in range(second, second + GROUP):
                    partner = wide_ref[n]
                    back = jnp.zeros((16, LANES), jnp.float32) if first == 0 else pull_ref[n]
                    for i_m in range(GROUP):
                        term = entry(own[i_m], n) * (held[i_m] - partner)
                        pulls[i_m] += term
                        back -= term
                    pull_ref[n] = back
            for i_m in range(GROUP):
                toward = (held[i_m] - target) * entry(own[i_m], count)
                there = pl.ds(pl.multiple_of(own[i_m] % local * rows + i * 16, 16), 16)
                out_ref[slot[own[i_m] // local], there, :] = weight * (toward - pulls[i_m] * share)
        return carry

    lax.fori_loop(0, rows // 16, slab, 0)


def restore_kernel(degrees, lines, x_ref, out_ref, held_ref, sems):
    local, each, _ = held_ref.shape
    channels = x_ref.shape[0]
    rows = each // channels
    run = rows // lines
    copies = []
    for m in range(local):
        for c in range(channels):
            factor = jnp.exp2(-x_ref[c, local * rows : local * rows + 1, :]) * (2.0 * degrees)
            for line in range(lines):
                at = m * rows + line * run
                to = (line * channels + c) * run
                held_ref[m, to : to + run, :] = x_ref[c, at : at + run, :] * factor
        copy = pltpu.make_async_copy(held_ref.at[m], out_ref.at[pl.ds(m * each, each)], sems.at[m])
        copy.start()
        copies.append(copy)
    for copy in copies:
        copy.wait()


def on_device(members, observed, pair_order, degree_weight, cotangent):
    groups = lax.axis_size("member")
    spread = lax.axis_size("order")
    local, lines, channels, parts, slots = members.shape
    count = local * groups
    tiles = slots // LANES
    rows = lines * parts * tiles
    degrees = degree_weight.shape[0]
    shifts = (0, 4, 6, 2, 5, 7, 1, 3)
    stages = [[0, 1, 2], [3], [4], [5, 6], [7]]
    plans, place, entries = pair_table(stages, local, count)
    vmem = pltpu.CompilerParams(vmem_limit_bytes=16 << 20)
    whole = pl.BlockSpec(memory_space=pltpu.VMEM)
    outside = pl.BlockSpec(memory_space=pltpu.HBM)

    surface = jax.ShapeDtypeStruct((rows, LANES), jnp.float32)
    *sent, target, weights, drawn = pl.pallas_call(
        functools.partial(prepare_kernel, degrees, shifts),
        out_shape=(jax.ShapeDtypeStruct((local, lines, parts, slots), members.dtype),) * channels
        + (jax.ShapeDtypeStruct((lines, parts, slots), observed.dtype), surface, surface),
        in_specs=[outside] * 5,
        out_specs=(whole,) * (channels + 3),
        scratch_shapes=[
            pltpu.VMEM((local, lines, channels, parts, slots), members.dtype),
            pltpu.SMEM(pair_order.shape, jnp.int32),
            pltpu.VMEM(degree_weight.shape, jnp.float32),
            pltpu.SMEM(cotangent.shape, jnp.float32),
            pltpu.SemaphoreType.DMA((local,)),
            pltpu.SemaphoreType.DMA((local, channels)),
            pltpu.SemaphoreType.DMA((4,)),
        ],
        compiler_params=vmem,
        name="prepare",
    )(*(pltpu.with_memory_space_constraint(x, pltpu.HBM) for x in (members, observed, pair_order, degree_weight, cotangent)))
    target = as_rows(target).reshape(rows, LANES)
    held = [as_rows(sent[0]).reshape(local, rows, LANES)]
    for step in range(1, groups):
        block = sent[step]
        if step > 5:
            block, held[1] = lax.optimization_barrier((block, held[1]))
        block = lax.ppermute(block, "member", [(i, i ^ shifts[step]) for i in range(groups)])
        held.append(as_rows(block).reshape(local, rows, LANES))

    scaled, sums, against = [], [], target
    for stage, (plan, height) in zip(stages, plans):
        first, last = stage is stages[0], stage is stages[-1]
        fresh = [held[g] for g in stage]
        before = sums if last else []
        block = jax.ShapeDtypeStruct((local, rows, LANES), jnp.float32)
        lead = jax.ShapeDtypeStruct((8 if last else height, LANES), jnp.float32)
        result = pl.pallas_call(
            functools.partial(distance_kernel, plan, len(scaled), len(fresh), len(before), first, last),
            out_shape=(lead,) + (block,) * len(fresh) + ((surface,) if first else ()),
            scratch_shapes=[pltpu.VMEM((height * LANES, LANES), jnp.float32)],
            compiler_params=vmem,
            name="distances",
        )(*scaled, *fresh, against, weights, *before)
        sums = sums + [result[0]]
        scaled = scaled + list(result[1 : 1 + len(fresh)])
        if first:
            against = result[-1]
    got = lax.all_to_all(jnp.broadcast_to(sums[-1][None], (spread, 8, LANES)), "order", 0, 0, tiled=True)

    gradient = pl.pallas_call(
        functools.partial(gradient_kernel, place, count, shifts),
        out_shape=jax.ShapeDtypeStruct((groups, local * rows + 16, LANES), jnp.float32),
        scratch_shapes=[
            pltpu.VMEM((entries, LANES), jnp.float32),
            pltpu.VMEM((count, 16, LANES), jnp.float32),
            pltpu.VMEM((count, 16, LANES), jnp.float32),
        ],
        compiler_params=vmem,
        name="gradients",
    )(got, *held, target, drawn)

    back = lax.all_to_all(gradient.astype(jnp.float16), "member", 0, 0, tiled=True).astype(jnp.float32)
    back = pl.pallas_call(
        functools.partial(restore_kernel, degrees, lines),
        out_shape=jax.ShapeDtypeStruct((local * rows * channels, LANES), jnp.float32),
        in_specs=[whole],
        out_specs=outside,
        scratch_shapes=[
            pltpu.VMEM((local, rows * channels, LANES), jnp.float32),
            pltpu.SemaphoreType.DMA((local,)),
        ],
        compiler_params=vmem,
        name="restore",
    )(back)
    return from_rows(back.reshape(local * lines * channels, tiles, parts, LANES)).reshape(members.shape)


def as_rows(block):
    parts, slots = block.shape[-2:]
    split = block.reshape(-1, parts, slots // LANES, LANES)
    return with_layout_constraint(split, Layout((0, 2, 1, 3))).transpose(0, 2, 1, 3)


def from_rows(block):
    count, tiles, parts, lanes = block.shape
    split = with_layout_constraint(block.transpose(0, 2, 1, 3), Layout((0, 2, 1, 3)))
    return split.reshape(count, parts, tiles * lanes)


def solution(mesh):
    placed = (
        P("member", "order", None, None, None),
        P("order", None, None, None),
        P("order"),
        P(),
        P(),
    )
    return jax.shard_map(
        on_device,
        mesh=mesh,
        in_specs=placed,
        out_specs=P("member", "order", None, None, None),
        check_vma=False,
    )
```

```python
import functools

import jax
import jax.numpy as jnp
from jax import lax
from jax.experimental import pallas as pl
from jax.experimental.layout import Layout, with_layout_constraint
from jax.experimental.pallas import tpu as pltpu
from jax.sharding import PartitionSpec as P

epsilon = 1e-06
LANES = 128
GROUP = 4
BATCH = 32
POWER = 13.0


def pair_table(stages, local, count):
    members_of = [list(range(g * local, (g + 1) * local)) for g in range(count // local)]
    plans, place, start = [], {}, 0
    for stage in stages:
        cross = [(a, b) for b in stage for a in range(b)]
        lists = [
            [(m, n) for a, b in cross[at : at + 2] for m in members_of[a] for n in members_of[b]]
            for at in range(0, len(cross), 2)
        ]
        for at in range(0, len(stage), 2):
            own = [members_of[g] for g in stage[at : at + 2]]
            inner = [(m, n) for g in own for i, m in enumerate(g) for n in g[i + 1 :]]
            lists.append(inner + [(m, count) for g in own for m in g])
        if len(lists) > 1 and len(lists[-1]) + len(lists[-2]) <= BATCH:
            lists[-2:] = [lists[-2] + lists[-1]]
        plan, first = [], start
        for batch in lists:
            plan.append((batch, start - first))
            for index, pair in enumerate(batch):
                place[pair] = start + index
            start += -(-len(batch) // 8) * 8
        start = -(-start // LANES) * LANES
        plans.append((plan, (start - first) // LANES))
    return plans, place, start


def fold_rows(blocks):
    row = lax.broadcasted_iota(jnp.int32, (8, LANES), 0)
    for half in (4, 2, 1):
        low = (row & half) == 0
        count = len(blocks) // 2
        merged = []
        for i in range(count):
            a, b = blocks[i], blocks[i + count]
            kept = jnp.where(low, a, b)
            moved = jnp.where(low, b, a)
            merged.append(kept + (pltpu.roll(moved, half, 0) if half == 4 else swap(moved, half, low)))
        blocks = merged
    return blocks[0]


def swap(block, half, low):
    return jnp.where(low, pltpu.roll(block, 8 - half, 0), pltpu.roll(block, half, 0))


def prepare_kernel(degrees, shifts, x_ref, y_ref, order_from, table_from, c_from, *refs):
    *out_refs, target_ref, weight_ref, drawn_ref, near_ref, order_ref, table_ref, c_ref, in_sems, out_sems, sems = refs
    local = near_ref.shape[0]
    me = lax.axis_index("member")
    into = [pltpu.make_async_copy(x_ref.at[m], near_ref.at[m], in_sems.at[m]) for m in range(local)]
    small = [
        pltpu.make_async_copy(order_from, order_ref, sems.at[0]),
        pltpu.make_async_copy(table_from, table_ref, sems.at[1]),
        pltpu.make_async_copy(c_from, c_ref, sems.at[2]),
        pltpu.make_async_copy(y_ref.at[:, me], target_ref, sems.at[3]),
    ]
    for copy in into + small:
        copy.start()
    out = []
    for m in range(local):
        into[m].wait()
        for step, shift in enumerate(shifts):
            channel = jnp.bitwise_xor(me, shift)
            copy = pltpu.make_async_copy(near_ref.at[m, :, channel], out_refs[step].at[m], out_sems.at[m, step])
            copy.start()
            out.append(copy)
    for copy in small:
        copy.wait()

    parts = target_ref.shape[-1] // LANES
    slots = parts * LANES
    line = table_ref[...].reshape(1, degrees)
    line = jnp.concatenate([line, jnp.zeros((1, slots - degrees), jnp.float32)], axis=1)
    table = jnp.broadcast_to(line, (8, slots))
    slot = lax.broadcasted_iota(jnp.int32, table.shape, 1)
    tail = pltpu.roll(table, 1, 1)
    half = 0.5 * c_ref[me]
    for row in range(order_ref.shape[0]):
        order = order_ref[row]
        head = pltpu.roll(table, lax.rem(slots - jnp.maximum(order, 0), slots), 1)
        leading = slot < degrees - order
        second = (slot <= degrees) & (2 * order < degrees - 1)
        usable = (order >= 0) & (leading | second)
        times = jnp.where(leading & (order == 0), 1.0, 2.0)
        line = jnp.where(usable, jnp.where(leading, head, tail) * times, 0.0)
        for part in range(parts):
            at = (row * parts + part) * 2
            piece = line[0:2, part * LANES : (part + 1) * LANES]
            weight_ref[at : at + 2, :] = piece
            drawn_ref[at : at + 2, :] = piece * half
    for copy in out:
        copy.wait()


def distance_kernel(plan, blocks, fresh, earlier, with_target, last, *refs):
    refs = list(refs)
    old_refs = [refs.pop(0) for _ in range(blocks)]
    new_refs = [refs.pop(0) for _ in range(fresh)]
    y_ref, w_ref = refs.pop(0), refs.pop(0)
    before = [refs.pop(0) for _ in range(earlier)]
    line_ref = refs.pop(0)
    scaled_refs = [refs.pop(0) for _ in range(fresh)]
    target_ref = refs.pop(0) if with_target else y_ref
    sums_ref = refs.pop(0)
    rows = w_ref.shape[0]
    local = new_refs[0].shape[0]

    def scale(i, carry):
        at = pl.ds(pl.multiple_of(i * 16, 16), 16)
        root = jnp.sqrt(w_ref[at, :])
        for x_ref, scaled_ref in zip(new_refs, scaled_refs):
            for m in range(local):
                scaled_ref[m, at, :] = x_ref[m, at, :].astype(jnp.float32) * root
        if with_target:
            target_ref[at, :] = y_ref[at, :].astype(jnp.float32) * root
        return carry

    lax.fori_loop(0, rows // 16, scale, 0)
    every = old_refs + scaled_refs

    def piece(m, at):
        if m // local < blocks + fresh:
            return every[m // local][m % local, at : at + 8, :]
        return target_ref[at : at + 8, :]

    zero = jnp.zeros((8, LANES), jnp.float32)
    sums_ref[...] = jnp.zeros_like(sums_ref)
    for batch, start in plan:
        used = sorted({m for pair in batch for m in pair})
        sums = [zero] * len(batch)
        for at in range(0, rows, 8):
            held = {m: piece(m, at) for m in used}
            for index, (m, n) in enumerate(batch):
                difference = held[m] - held[n]
                sums[index] = sums[index] + difference * difference
        sums += [zero] * (-len(sums) % 8)
        for at in range(0, len(sums), 8):
            sums_ref[start + at : start + at + 8, :] = fold_rows(sums[at : at + 8])
    to = 0
    if last:
        line_ref[...] = jnp.zeros_like(line_ref)
        for ref in before:
            line_ref[to : to + ref.shape[0], :] = ref[...]
            to += ref.shape[0]
    for block in range(sums_ref.shape[0] // LANES):
        square = sums_ref[block * LANES : (block + 1) * LANES, :].T
        line_ref[to + block : to + block + 1, :] = jnp.sum(square, axis=0, keepdims=True)


def gradient_kernel(place, count, turn, rest, first, *refs):
    refs = list(refs)
    from_refs = [refs.pop(0) for _ in range(1 if first else 2)]
    x_refs = [refs.pop(0) for _ in range(count // GROUP)]
    y_ref, w_ref = refs.pop(0), refs.pop(0)
    before = {} if first else {g: refs.pop(0) for g in turn}
    out_refs = {g: refs.pop(0) for g in turn}
    after = {g: refs.pop(0) for g in rest}
    if first:
        table_ref, power_ref, wide_ref, pull_ref = refs
        squares = jnp.sum(from_refs[0][...], axis=0)
        inverse = lax.rsqrt(squares + epsilon)
        largest = jnp.max(squares * inverse * inverse, axis=(0, 1), keepdims=True)
        power = POWER + jnp.floor(jnp.clip(-0.5 * jnp.log2(jnp.maximum(largest, 1e-30)), 0.0, 50.0))
        power = jnp.broadcast_to(power, (16, LANES))
        power_ref[...] = power
        columns = inverse.T
        for block in range(table_ref.shape[0] // LANES):
            column = jnp.broadcast_to(columns[:, block : block + 1], (LANES, LANES))
            table_ref[block * LANES : (block + 1) * LANES, :] = column
    else:
        wide_ref, pull_ref = refs
        table_ref = from_refs[0]
        power = from_refs[1][...]
    rows = w_ref.shape[0]
    scale = jnp.exp2(power)
    for g in turn:
        out_refs[g][GROUP * rows :, :] = power

    def entry(m, n):
        at = place[(min(m, n), max(m, n))]
        return jnp.broadcast_to(table_ref[at : at + 1, :], (16, LANES))

    def slab(i, carry):
        at = pl.ds(pl.multiple_of(i * 16, 16), 16)
        for g in turn + rest:
            for k in range(GROUP):
                wide_ref[g * GROUP + k] = x_refs[g][k, at, :].astype(jnp.float32)
        target = y_ref[at, :].astype(jnp.float32)
        weight = w_ref[at, :] * scale
        share = 1.0 / (count - 1)
        zero = jnp.zeros((16, LANES), jnp.float32)
        fresh = {g: not before for g in turn + rest}
        for index, g in enumerate(turn):
            own = list(range(g * GROUP, (g + 1) * GROUP))
            held = [wide_ref[m] for m in own]
            if fresh[g]:
                pulls = [zero] * GROUP
            elif index == 0:
                pulls = [before[g][k, at, :] for k in range(GROUP)]
            else:
                pulls = [pull_ref[m] for m in own]
            for i_m in range(GROUP):
                for i_n in range(i_m + 1, GROUP):
                    term = entry(own[i_m], own[i_n]) * (held[i_m] - held[i_n])
                    pulls[i_m] += term
                    pulls[i_n] -= term
            for h in turn[index + 1 :] + rest:
                for k in range(GROUP):
                    n = h * GROUP + k
                    partner = wide_ref[n]
                    if fresh[h]:
                        back = zero
                    elif index == 0:
                        back = before[h][k, at, :]
                    else:
                        back = pull_ref[n]
                    for i_m in range(GROUP):
                        term = entry(own[i_m], n) * (held[i_m] - partner)
                        pulls[i_m] += term
                        back -= term
                    if h in after and index == len(turn) - 1:
                        after[h][k, at, :] = back
                    else:
                        pull_ref[n] = back
                fresh[h] = False
            for k in range(GROUP):
                toward = (held[k] - target) * entry(own[k], count)
                there = pl.ds(pl.multiple_of(k * rows + i * 16, 16), 16)
                out_refs[g][there, :] = weight * (toward - pulls[k] * share)
        return carry

    lax.fori_loop(0, rows // 16, slab, 0)


def restore_kernel(degrees, lines, shifts, *refs):
    *x_refs, out_ref, held_ref, sems = refs
    local, each, _ = held_ref.shape
    channels = len(x_refs)
    rows = each // channels
    run = rows // lines
    me = lax.axis_index("member")
    copies = []
    for m in range(local):
        for x_ref, shift in zip(x_refs, shifts):
            factor = jnp.exp2(-x_ref[local * rows : local * rows + 1, :]) * (2.0 * degrees)
            for line in range(lines):
                at = m * rows + line * run
                to = pl.multiple_of(line * channels * run + jnp.bitwise_xor(me, shift) * run, 4)
                held_ref[m, pl.ds(to, run), :] = x_ref[at : at + run, :] * factor
        copy = pltpu.make_async_copy(held_ref.at[m], out_ref.at[pl.ds(m * each, each)], sems.at[m])
        copy.start()
        copies.append(copy)
    for copy in copies:
        copy.wait()


def on_device(members, observed, pair_order, degree_weight, cotangent):
    groups = lax.axis_size("member")
    spread = lax.axis_size("order")
    local, lines, channels, parts, slots = members.shape
    count = local * groups
    tiles = slots // LANES
    rows = lines * parts * tiles
    degrees = degree_weight.shape[0]
    shifts = (0, 4, 6, 2, 5, 7, 1, 3)
    turns = [[1, 2, 4], [6, 7, 3, 5, 0]]
    stages = [[0, 1, 2], [3], [4, 5], [6, 7]]
    plans, place, entries = pair_table(stages, local, count)
    vmem = pltpu.CompilerParams(vmem_limit_bytes=16 << 20)
    whole = pl.BlockSpec(memory_space=pltpu.VMEM)
    outside = pl.BlockSpec(memory_space=pltpu.HBM)

    surface = jax.ShapeDtypeStruct((rows, LANES), jnp.float32)
    *sent, target, weights, drawn = pl.pallas_call(
        functools.partial(prepare_kernel, degrees, shifts),
        out_shape=(jax.ShapeDtypeStruct((local, lines, parts, slots), members.dtype),) * channels
        + (jax.ShapeDtypeStruct((lines, parts, slots), observed.dtype), surface, surface),
        in_specs=[outside] * 5,
        out_specs=(whole,) * (channels + 3),
        scratch_shapes=[
            pltpu.VMEM((local, lines, channels, parts, slots), members.dtype),
            pltpu.SMEM(pair_order.shape, jnp.int32),
            pltpu.VMEM(degree_weight.shape, jnp.float32),
            pltpu.SMEM(cotangent.shape, jnp.float32),
            pltpu.SemaphoreType.DMA((local,)),
            pltpu.SemaphoreType.DMA((local, channels)),
            pltpu.SemaphoreType.DMA((4,)),
        ],
        compiler_params=vmem,
        name="prepare",
    )(*(pltpu.with_memory_space_constraint(x, pltpu.HBM) for x in (members, observed, pair_order, degree_weight, cotangent)))
    target = as_rows(target).reshape(rows, LANES)
    held = [as_rows(sent[0]).reshape(local, rows, LANES)]
    for step in range(1, groups):
        block = sent[step]
        if step > 5:
            block, held[1] = lax.optimization_barrier((block, held[1]))
        block = lax.ppermute(block, "member", [(i, i ^ shifts[step]) for i in range(groups)])
        held.append(as_rows(block).reshape(local, rows, LANES))

    scaled, sums, against = [], [], target
    for stage, (plan, height) in zip(stages, plans):
        first, last = stage is stages[0], stage is stages[-1]
        fresh = [held[g] for g in stage]
        before = sums if last else []
        block = jax.ShapeDtypeStruct((local, rows, LANES), jnp.float32)
        lead = jax.ShapeDtypeStruct((8 if last else height, LANES), jnp.float32)
        result = pl.pallas_call(
            functools.partial(distance_kernel, plan, len(scaled), len(fresh), len(before), first, last),
            out_shape=(lead,) + (block,) * len(fresh) + ((surface,) if first else ()),
            scratch_shapes=[pltpu.VMEM((height * LANES, LANES), jnp.float32)],
            compiler_params=vmem,
            name="distances",
        )(*scaled, *fresh, against, weights, *before)
        sums = sums + [result[0]]
        scaled = scaled + list(result[1 : 1 + len(fresh)])
        if first:
            against = result[-1]
    pair = sums[-1] + lax.ppermute(sums[-1], "order", [(i, i ^ 1) for i in range(spread)])
    alike = [list(range(core, spread, 2)) for core in range(2)]
    got = jnp.broadcast_to(pair[None], (spread // 2, 8, LANES))
    got = lax.all_to_all(got, "order", 0, 0, tiled=True, axis_index_groups=alike)

    back, source, pulled = [None] * groups, (got,), {}
    for turn in turns:
        first = not pulled
        rest = [g for g in range(groups) if g not in turn] if first else []
        result = pl.pallas_call(
            functools.partial(gradient_kernel, place, count, turn, rest, first),
            out_shape=(jax.ShapeDtypeStruct((local * rows + 16, LANES), jnp.float32),) * len(turn)
            + (jax.ShapeDtypeStruct((local, rows, LANES), jnp.float32),) * len(rest)
            + ((jax.ShapeDtypeStruct((entries, LANES), jnp.float32), jax.ShapeDtypeStruct((16, LANES), jnp.float32)) if first else ()),
            scratch_shapes=[
                pltpu.VMEM((count, 16, LANES), jnp.float32),
                pltpu.VMEM((count, 16, LANES), jnp.float32),
            ],
            compiler_params=vmem,
            name="gradients",
        )(*source, *held, target, drawn, *(pulled[g] for g in turn if not first))
        if first:
            pulled = dict(zip(rest, result[len(turn) :]))
            source = result[-2:]
        for g, block in zip(turn, result):
            if shifts[g]:
                block = lax.ppermute(block.astype(jnp.float16), "member", [(i, i ^ shifts[g]) for i in range(groups)])
            back[g] = block.astype(jnp.float32)
    back = pl.pallas_call(
        functools.partial(restore_kernel, degrees, lines, shifts),
        out_shape=jax.ShapeDtypeStruct((local * rows * channels, LANES), jnp.float32),
        out_specs=outside,
        scratch_shapes=[
            pltpu.VMEM((local, rows * channels, LANES), jnp.float32),
            pltpu.SemaphoreType.DMA((local,)),
        ],
        compiler_params=vmem,
        name="restore",
    )(*back)
    return from_rows(back.reshape(local * lines * channels, tiles, parts, LANES)).reshape(members.shape)


def as_rows(block):
    parts, slots = block.shape[-2:]
    split = block.reshape(-1, parts, slots // LANES, LANES)
    return with_layout_constraint(split, Layout((0, 2, 1, 3))).transpose(0, 2, 1, 3)


def from_rows(block):
    count, tiles, parts, lanes = block.shape
    split = with_layout_constraint(block.transpose(0, 2, 1, 3), Layout((0, 2, 1, 3)))
    return split.reshape(count, parts, tiles * lanes)


def solution(mesh):
    placed = (
        P("member", "order", None, None, None),
        P("order", None, None, None),
        P("order"),
        P(),
        P(),
    )
    return jax.shard_map(
        on_device,
        mesh=mesh,
        in_specs=placed,
        out_specs=P("member", "order", None, None, None),
        check_vma=False,
    )
```

```python
import functools

import jax
import jax.numpy as jnp
from jax import lax
from jax.experimental import pallas as pl
from jax.experimental.layout import Layout, with_layout_constraint
from jax.experimental.pallas import tpu as pltpu
from jax.sharding import PartitionSpec as P

epsilon = 1e-06
LANES = 128
GROUP = 4
BATCH = 32
POWER = 13.0


def pair_table(stages, local, count):
    members_of = [list(range(g * local, (g + 1) * local)) for g in range(count // local)]
    plans, place, start = [], {}, 0
    for stage in stages:
        cross = [(a, b) for b in stage for a in range(b)]
        lists = [
            [(m, n) for a, b in cross[at : at + 2] for m in members_of[a] for n in members_of[b]]
            for at in range(0, len(cross), 2)
        ]
        for at in range(0, len(stage), 2):
            own = [members_of[g] for g in stage[at : at + 2]]
            inner = [(m, n) for g in own for i, m in enumerate(g) for n in g[i + 1 :]]
            lists.append(inner + [(m, count) for g in own for m in g])
        if len(lists) > 1 and len(lists[-1]) + len(lists[-2]) <= BATCH:
            lists[-2:] = [lists[-2] + lists[-1]]
        plan, first = [], start
        for batch in lists:
            plan.append((batch, start - first))
            for index, pair in enumerate(batch):
                place[pair] = start + index
            start += -(-len(batch) // 8) * 8
        start = -(-start // LANES) * LANES
        plans.append((plan, (start - first) // LANES))
    return plans, place, start


def fold_rows(blocks):
    row = lax.broadcasted_iota(jnp.int32, (8, LANES), 0)
    for half in (4, 2, 1):
        low = (row & half) == 0
        count = len(blocks) // 2
        merged = []
        for i in range(count):
            a, b = blocks[i], blocks[i + count]
            kept = jnp.where(low, a, b)
            moved = jnp.where(low, b, a)
            merged.append(kept + (pltpu.roll(moved, half, 0) if half == 4 else swap(moved, half, low)))
        blocks = merged
    return blocks[0]


def swap(block, half, low):
    return jnp.where(low, pltpu.roll(block, 8 - half, 0), pltpu.roll(block, half, 0))


def prepare_kernel(degrees, shifts, x_ref, y_ref, order_from, table_from, c_from, *refs):
    *out_refs, target_ref, weight_ref, drawn_ref, near_ref, order_ref, table_ref, c_ref, in_sems, out_sems, sems = refs
    local = near_ref.shape[0]
    me = lax.axis_index("member")
    into = [pltpu.make_async_copy(x_ref.at[m], near_ref.at[m], in_sems.at[m]) for m in range(local)]
    small = [
        pltpu.make_async_copy(order_from, order_ref, sems.at[0]),
        pltpu.make_async_copy(table_from, table_ref, sems.at[1]),
        pltpu.make_async_copy(c_from, c_ref, sems.at[2]),
        pltpu.make_async_copy(y_ref.at[:, me], target_ref, sems.at[3]),
    ]
    for copy in into + small:
        copy.start()
    out = []
    for m in range(local):
        into[m].wait()
        for step, shift in enumerate(shifts):
            channel = jnp.bitwise_xor(me, shift)
            copy = pltpu.make_async_copy(near_ref.at[m, :, channel], out_refs[step].at[m], out_sems.at[m, step])
            copy.start()
            out.append(copy)
    for copy in small:
        copy.wait()

    parts = target_ref.shape[-1] // LANES
    slots = parts * LANES
    line = table_ref[...].reshape(1, degrees)
    line = jnp.concatenate([line, jnp.zeros((1, slots - degrees), jnp.float32)], axis=1)
    table = jnp.broadcast_to(line, (8, slots))
    slot = lax.broadcasted_iota(jnp.int32, table.shape, 1)
    tail = pltpu.roll(table, 1, 1)
    half = 0.5 * c_ref[me]
    for row in range(order_ref.shape[0]):
        order = order_ref[row]
        head = pltpu.roll(table, lax.rem(slots - jnp.maximum(order, 0), slots), 1)
        leading = slot < degrees - order
        second = (slot <= degrees) & (2 * order < degrees - 1)
        usable = (order >= 0) & (leading | second)
        times = jnp.where(leading & (order == 0), 1.0, 2.0)
        line = jnp.where(usable, jnp.where(leading, head, tail) * times, 0.0)
        for part in range(parts):
            at = (row * parts + part) * 2
            piece = line[0:2, part * LANES : (part + 1) * LANES]
            weight_ref[at : at + 2, :] = piece
            drawn_ref[at : at + 2, :] = jnp.sqrt(piece) * half
    for copy in out:
        copy.wait()


def distance_kernel(plan, blocks, fresh, earlier, with_target, last, *refs):
    refs = list(refs)
    old_refs = [refs.pop(0) for _ in range(blocks)]
    new_refs = [refs.pop(0) for _ in range(fresh)]
    y_ref, w_ref = refs.pop(0), refs.pop(0)
    before = [refs.pop(0) for _ in range(earlier)]
    line_ref = refs.pop(0)
    scaled_refs = [refs.pop(0) for _ in range(fresh)]
    target_ref = refs.pop(0) if with_target else y_ref
    sums_ref = refs.pop(0)
    rows = w_ref.shape[0]
    local = new_refs[0].shape[0]

    def scale(i, carry):
        at = pl.ds(pl.multiple_of(i * 16, 16), 16)
        root = jnp.sqrt(w_ref[at, :])
        for x_ref, scaled_ref in zip(new_refs, scaled_refs):
            for m in range(local):
                scaled_ref[m, at, :] = x_ref[m, at, :].astype(jnp.float32) * root
        if with_target:
            target_ref[at, :] = y_ref[at, :].astype(jnp.float32) * root
        return carry

    lax.fori_loop(0, rows // 16, scale, 0)
    every = old_refs + scaled_refs

    def piece(m, at):
        if m // local < blocks + fresh:
            return every[m // local][m % local, at : at + 8, :]
        return target_ref[at : at + 8, :]

    zero = jnp.zeros((8, LANES), jnp.float32)
    sums_ref[...] = jnp.zeros_like(sums_ref)
    for batch, start in plan:
        used = sorted({m for pair in batch for m in pair})
        sums = [zero] * len(batch)
        for at in range(0, rows, 8):
            held = {m: piece(m, at) for m in used}
            for index, (m, n) in enumerate(batch):
                difference = held[m] - held[n]
                sums[index] = sums[index] + difference * difference
        sums += [zero] * (-len(sums) % 8)
        for at in range(0, len(sums), 8):
            sums_ref[start + at : start + at + 8, :] = fold_rows(sums[at : at + 8])
    to = 0
    if last:
        line_ref[...] = jnp.zeros_like(line_ref)
        for ref in before:
            line_ref[to : to + ref.shape[0], :] = ref[...]
            to += ref.shape[0]
    for block in range(sums_ref.shape[0] // LANES):
        square = sums_ref[block * LANES : (block + 1) * LANES, :].T
        line_ref[to + block : to + block + 1, :] = jnp.sum(square, axis=0, keepdims=True)


def gradient_kernel(place, count, turn, rest, first, *refs):
    refs = list(refs)
    from_refs = [refs.pop(0) for _ in range(1 if first else 2)]
    x_refs = [refs.pop(0) for _ in range(count // GROUP)]
    y_ref, w_ref = refs.pop(0), refs.pop(0)
    before = {} if first else {g: refs.pop(0) for g in turn}
    out_refs = {g: refs.pop(0) for g in turn}
    after = {g: refs.pop(0) for g in rest}
    if first:
        table_ref, power_ref, pull_ref = refs
        squares = jnp.sum(from_refs[0][...], axis=0)
        inverse = lax.rsqrt(squares + epsilon)
        largest = jnp.max(squares * inverse * inverse, axis=(0, 1), keepdims=True)
        power = POWER + jnp.floor(jnp.clip(-0.5 * jnp.log2(jnp.maximum(largest, 1e-30)), 0.0, 50.0))
        power = jnp.broadcast_to(power, (16, LANES))
        power_ref[...] = power
        columns = inverse.T
        for block in range(table_ref.shape[0] // LANES):
            column = jnp.broadcast_to(columns[:, block : block + 1], (LANES, LANES))
            table_ref[block * LANES : (block + 1) * LANES, :] = column
    else:
        (pull_ref,) = refs
        table_ref = from_refs[0]
        power = from_refs[1][...]
    rows = w_ref.shape[0]
    scale = jnp.exp2(power)
    for g in turn:
        out_refs[g][GROUP * rows :, :] = power

    def entry(m, n):
        at = place[(min(m, n), max(m, n))]
        return jnp.broadcast_to(table_ref[at : at + 1, :], (16, LANES))

    def slab(i):
        at = slice(i * 16, (i + 1) * 16)
        target = y_ref[at, :]
        weight = w_ref[at, :] * scale
        share = 1.0 / (count - 1)
        zero = jnp.zeros((16, LANES), jnp.float32)
        fresh = {g: not before for g in turn + rest}
        for index, g in enumerate(turn):
            own = list(range(g * GROUP, (g + 1) * GROUP))
            held = [x_refs[g][k, at, :] for k in range(GROUP)]
            if fresh[g]:
                pulls = [zero] * GROUP
            elif index == 0:
                pulls = [before[g][k, at, :] for k in range(GROUP)]
            else:
                pulls = [pull_ref[m] for m in own]
            for i_m in range(GROUP):
                for i_n in range(i_m + 1, GROUP):
                    term = entry(own[i_m], own[i_n]) * (held[i_m] - held[i_n])
                    pulls[i_m] += term
                    pulls[i_n] -= term
            for h in turn[index + 1 :] + rest:
                for k in range(GROUP):
                    n = h * GROUP + k
                    partner = x_refs[h][k, at, :]
                    if fresh[h]:
                        back = zero
                    elif index == 0:
                        back = before[h][k, at, :]
                    else:
                        back = pull_ref[n]
                    for i_m in range(GROUP):
                        term = entry(own[i_m], n) * (held[i_m] - partner)
                        pulls[i_m] += term
                        back -= term
                    if h in after and index == len(turn) - 1:
                        after[h][k, at, :] = back
                    else:
                        pull_ref[n] = back
                fresh[h] = False
            for k in range(GROUP):
                toward = (held[k] - target) * entry(own[k], count)
                there = slice(k * rows + i * 16, k * rows + (i + 1) * 16)
                out_refs[g][there, :] = weight * (toward - pulls[k] * share)

    for i in range(rows // 16):
        slab(i)


def restore_kernel(degrees, lines, shifts, *refs):
    *x_refs, out_ref, held_ref, sems = refs
    local, each, _ = held_ref.shape
    channels = len(x_refs)
    rows = each // channels
    run = rows // lines
    me = lax.axis_index("member")
    copies = []
    for m in range(local):
        for x_ref, shift in zip(x_refs, shifts):
            factor = jnp.exp2(-x_ref[local * rows : local * rows + 1, :]) * (2.0 * degrees)
            for line in range(lines):
                at = m * rows + line * run
                to = pl.multiple_of(line * channels * run + jnp.bitwise_xor(me, shift) * run, 4)
                held_ref[m, pl.ds(to, run), :] = x_ref[at : at + run, :] * factor
        copy = pltpu.make_async_copy(held_ref.at[m], out_ref.at[pl.ds(m * each, each)], sems.at[m])
        copy.start()
        copies.append(copy)
    for copy in copies:
        copy.wait()


def on_device(members, observed, pair_order, degree_weight, cotangent):
    groups = lax.axis_size("member")
    spread = lax.axis_size("order")
    local, lines, channels, parts, slots = members.shape
    count = local * groups
    tiles = slots // LANES
    rows = lines * parts * tiles
    degrees = degree_weight.shape[0]
    shifts = (0, 4, 6, 2, 5, 7, 1, 3)
    turns = [[1, 2, 4], [6, 7, 3, 5, 0]]
    stages = [[0, 1, 2], [3], [4, 5], [6, 7]]
    plans, place, entries = pair_table(stages, local, count)
    vmem = pltpu.CompilerParams(vmem_limit_bytes=16 << 20)
    whole = pl.BlockSpec(memory_space=pltpu.VMEM)
    outside = pl.BlockSpec(memory_space=pltpu.HBM)

    surface = jax.ShapeDtypeStruct((rows, LANES), jnp.float32)
    *sent, target, weights, drawn = pl.pallas_call(
        functools.partial(prepare_kernel, degrees, shifts),
        out_shape=(jax.ShapeDtypeStruct((local, lines, parts, slots), members.dtype),) * channels
        + (jax.ShapeDtypeStruct((lines, parts, slots), observed.dtype), surface, surface),
        in_specs=[outside] * 5,
        out_specs=(whole,) * (channels + 3),
        scratch_shapes=[
            pltpu.VMEM((local, lines, channels, parts, slots), members.dtype),
            pltpu.SMEM(pair_order.shape, jnp.int32),
            pltpu.VMEM(degree_weight.shape, jnp.float32),
            pltpu.SMEM(cotangent.shape, jnp.float32),
            pltpu.SemaphoreType.DMA((local,)),
            pltpu.SemaphoreType.DMA((local, channels)),
            pltpu.SemaphoreType.DMA((4,)),
        ],
        compiler_params=vmem,
        name="prepare",
    )(*(pltpu.with_memory_space_constraint(x, pltpu.HBM) for x in (members, observed, pair_order, degree_weight, cotangent)))
    target = as_rows(target).reshape(rows, LANES)
    held = [as_rows(sent[0]).reshape(local, rows, LANES)]
    for step in range(1, groups):
        block = sent[step]
        if step > 5:
            block, held[1] = lax.optimization_barrier((block, held[1]))
        block = lax.ppermute(block, "member", [(i, i ^ shifts[step]) for i in range(groups)])
        held.append(as_rows(block).reshape(local, rows, LANES))

    scaled, sums, against = [], [], target
    for stage, (plan, height) in zip(stages, plans):
        first, last = stage is stages[0], stage is stages[-1]
        fresh = [held[g] for g in stage]
        before = sums if last else []
        block = jax.ShapeDtypeStruct((local, rows, LANES), jnp.float32)
        lead = jax.ShapeDtypeStruct((8 if last else height, LANES), jnp.float32)
        result = pl.pallas_call(
            functools.partial(distance_kernel, plan, len(scaled), len(fresh), len(before), first, last),
            out_shape=(lead,) + (block,) * len(fresh) + ((surface,) if first else ()),
            scratch_shapes=[pltpu.VMEM((height * LANES, LANES), jnp.float32)],
            compiler_params=vmem,
            name="distances",
        )(*scaled, *fresh, against, weights, *before)
        sums = sums + [result[0]]
        scaled = scaled + list(result[1 : 1 + len(fresh)])
        if first:
            against = result[-1]
    pair = sums[-1] + lax.ppermute(sums[-1], "order", [(i, i ^ 1) for i in range(spread)])
    alike = [list(range(core, spread, 2)) for core in range(2)]
    got = jnp.broadcast_to(pair[None], (spread // 2, 8, LANES))
    got = lax.all_to_all(got, "order", 0, 0, tiled=True, axis_index_groups=alike)

    back, source, pulled = [None] * groups, (got,), {}
    for turn in turns:
        first = not pulled
        rest = [g for g in range(groups) if g not in turn] if first else []
        result = pl.pallas_call(
            functools.partial(gradient_kernel, place, count, turn, rest, first),
            out_shape=(jax.ShapeDtypeStruct((local * rows + 16, LANES), jnp.float32),) * len(turn)
            + (jax.ShapeDtypeStruct((local, rows, LANES), jnp.float32),) * len(rest)
            + ((jax.ShapeDtypeStruct((entries, LANES), jnp.float32), jax.ShapeDtypeStruct((16, LANES), jnp.float32)) if first else ()),
            scratch_shapes=[pltpu.VMEM((count, 16, LANES), jnp.float32)],
            compiler_params=vmem,
            name="gradients",
        )(*source, *scaled, against, drawn, *(pulled[g] for g in turn if not first))
        if first:
            pulled = dict(zip(rest, result[len(turn) :]))
            source = result[-2:]
        for g, block in zip(turn, result):
            if shifts[g]:
                block = lax.ppermute(block.astype(jnp.float16), "member", [(i, i ^ shifts[g]) for i in range(groups)])
            back[g] = block.astype(jnp.float32)
    back = pl.pallas_call(
        functools.partial(restore_kernel, degrees, lines, shifts),
        out_shape=jax.ShapeDtypeStruct((local * rows * channels, LANES), jnp.float32),
        out_specs=outside,
        scratch_shapes=[
            pltpu.VMEM((local, rows * channels, LANES), jnp.float32),
            pltpu.SemaphoreType.DMA((local,)),
        ],
        compiler_params=vmem,
        name="restore",
    )(*back)
    return from_rows(back.reshape(local * lines * channels, tiles, parts, LANES)).reshape(members.shape)


def as_rows(block):
    parts, slots = block.shape[-2:]
    split = block.reshape(-1, parts, slots // LANES, LANES)
    return with_layout_constraint(split, Layout((0, 2, 1, 3))).transpose(0, 2, 1, 3)


def from_rows(block):
    count, tiles, parts, lanes = block.shape
    split = with_layout_constraint(block.transpose(0, 2, 1, 3), Layout((0, 2, 1, 3)))
    return split.reshape(count, parts, tiles * lanes)


def solution(mesh):
    placed = (
        P("member", "order", None, None, None),
        P("order", None, None, None),
        P("order"),
        P(),
        P(),
    )
    return jax.shard_map(
        on_device,
        mesh=mesh,
        in_specs=placed,
        out_specs=P("member", "order", None, None, None),
        check_vma=False,
    )
```
